128 devices in a mesh: grp: 8 (over x_hi, y), tile: 16 (over x_lo, z, core).
Axes of the slice: x: 4 (x_hi: 2, x_lo: 2; x = x_hi * 2 + x_lo), y: 4, z: 4, core: 2. Of those that a mesh axis runs over, the one named last changes fastest.
Arguments:
- object_real: float32 [2, 1280, 2048], P(None, 'grp', 'tile'), may hold values from 0.6 to 1.2
- object_imag: float32 [2, 1280, 2048], P(None, 'grp', 'tile'), may hold values from -2.5 to 2.5
- probe_real: float32 [6, 128, 128], replicated, may hold values from -2.5 to 2.5
- probe_imag: float32 [6, 128, 128], replicated, may hold values from -2.5 to 2.5
- measured: float32 [8, 16, 4, 128, 128], P('grp', 'tile'), may hold values from 0 to 1
- scan_tiles: int32 [8, 16, 4], P('grp', 'tile'), may hold values from 0 to 14, as said below
- row_offsets: int32 [8, 16, 4], P('grp', 'tile'), may hold values from 0 to 32
- column_offsets: int32 [8, 16, 4], P('grp', 'tile'), may hold values from 0 to 127
- live_slots: int32 [8, 16], P('grp', 'tile'), may hold values from 1 to 4, as said below
Outputs:
- object_real_out: float32 [2, 1280, 2048], P(None, 'grp', 'tile')
- object_imag_out: float32 [2, 1280, 2048], P(None, 'grp', 'tile')
- probe_real_out: float32 [6, 128, 128], replicated
- probe_imag_out: float32 [6, 128, 128], replicated
The draws below stay inside these ranges and needn't reach their ends.
Inputs may be any that keep to these rules, and one draw needn't show every extreme that they name: scan_tiles[g, t, s] lies within 2 of t, so a window reads only tiles t - 2 to t + 3 of its row of tiles. `live_slots`: the live slots of a device are its first ones; in every row of tiles one device has all 4 slots live and each other device at least one and at most half of 4 (rounded down, but at least one).
All inputs are finite; a program needn't handle non-finite values.
Results may differ from the reference program's by a relative error of at most 0.0003.
Values sent between devices are 32-bit elements; how exact they have to be, the bound alone decides.
No kernel may reach another device: no remote copies, remote signals or barrier semaphores. Data moves between devices by JAX's collectives and lax.ppermute only.
A program may use at most 128 MiB of HBM per device.

```python
import jax
import jax.numpy as jnp
from jax import lax

N = 128
M = 6
SLICES = 2
ITERS = 2
REACH = 2
TH = 160
TW = 128
P_CAP = 4
GROUPS = 8
TILES = 16
OBJ_ROWS = 1280
OBJ_COLS = 2048


def draw_scan_tiles(key, part):
    key = jax.random.fold_in(key, 11)
    offset = jax.random.randint(key, (GROUPS, TILES, P_CAP), -REACH, REACH + 1)
    holder = jnp.arange(TILES, dtype=jnp.int32)[None, :, None]
    return jnp.clip(holder + offset, 0, TILES - 2).astype(jnp.int32)


def draw_live_slots(key, part):
    key = jax.random.fold_in(key, 23)
    first_key, second_key = jax.random.split(key)
    counts = jax.random.randint(first_key, (GROUPS, TILES), 1, max(P_CAP // 2, 1) + 1)
    busiest = jax.random.randint(second_key, (GROUPS, 1), 0, TILES)
    holder = jnp.arange(TILES, dtype=jnp.int32)[None, :]
    return jnp.where(holder == busiest, P_CAP, counts).astype(jnp.int32)


def with_ends(values, own_key, least, top_value):
    dims = values.shape
    place = [jax.random.randint(jax.random.fold_in(own_key, axis), (), 0, dims[axis]) for axis in range(len(dims))]
    values = values.at[tuple(place)].set(least)
    longest = dims.index(max(dims))
    place[longest] = (place[longest] + 1) % dims[longest]
    return values.at[tuple(place)].set(top_value)


def block_scale(rng, dims, cuts, low, largest):
    level = 1.0
    for position, parts in cuts:
        draws = jax.random.uniform(jax.random.fold_in(jax.random.fold_in(rng, 6), position), (parts,), jnp.float32, low / len(cuts), largest / len(cuts))
        level = level * jnp.repeat(jnp.exp(draws), dims[position] // parts).reshape((-1,) + (1,) * (len(dims) - 1 - position))
    return level


def centred(key, extent, scale, bound, cuts=(), kind=jnp.bfloat16):
    loudness = block_scale(key, extent, cuts, -0.22, 0.18) if cuts else 1.0
    result = jax.random.normal(key, extent, jnp.float32) * scale * loudness
    return jnp.minimum(jnp.maximum(result, -bound), bound).astype(kind)


def setup_inputs(seed: int = 0) -> dict:
    key_list = jax.random.split(jax.random.key(seed), 10)
    object_real = jnp.clip(0.6 + 0.6 * jax.random.uniform(key_list[0], (SLICES, OBJ_ROWS, OBJ_COLS), jnp.float32) ** block_scale(key_list[0], (SLICES, OBJ_ROWS, OBJ_COLS), ((1, 8), (2, 16)), -0.2, 0.2), 0.6, 1.2)
    object_imag = centred(key_list[1], (SLICES, OBJ_ROWS, OBJ_COLS), 0.3, 2.5, ((1, 8), (2, 16)), jnp.float32)
    probe_real = centred(key_list[2], (M, N, N), 0.3, 2.5, (), jnp.float32)
    probe_imag = centred(key_list[3], (M, N, N), 0.3, 2.5, (), jnp.float32)
    measured = jnp.clip(1.0 * jax.random.uniform(key_list[4], (GROUPS, TILES, P_CAP, N, N), jnp.float32) ** block_scale(key_list[4], (GROUPS, TILES, P_CAP, N, N), ((0, 8), (1, 16)), -0.2, 0.2), 0.0, 1.0)
    scan_tiles = draw_scan_tiles(jax.random.fold_in(key_list[9], 71), 0)
    row_offsets = with_ends(jax.random.randint(key_list[6], (GROUPS, TILES, P_CAP), 0, TH - N + 1), jax.random.fold_in(key_list[6], 1), 0, TH - N).astype(jnp.int32)
    column_offsets = with_ends(jax.random.randint(key_list[7], (GROUPS, TILES, P_CAP), 0, TW), jax.random.fold_in(key_list[7], 1), 0, TW - 1).astype(jnp.int32)
    live_slots = draw_live_slots(jax.random.fold_in(key_list[9], 71), 0)
    return dict(object_real=object_real, object_imag=object_imag, probe_real=probe_real, probe_imag=probe_imag, measured=measured, scan_tiles=scan_tiles, row_offsets=row_offsets, column_offsets=column_offsets, live_slots=live_slots)


FRESNEL = 20.0
OBJECT_STEP = 0.2
PROBE_STEP = 0.5


def fresnel_phase(width):
    index = jnp.arange(width, dtype=jnp.int32)
    signed = ((index + width // 2) % width - width // 2).astype(jnp.float32)
    phase = FRESNEL * (signed[:, None] ** 2 + signed[None, :] ** 2) / float(width * width)
    return jnp.stack([jnp.cos(phase), -jnp.sin(phase)])


def reference(object_real, object_imag, probe_real, probe_imag, measured, scan_tiles, row_offsets, column_offsets, live_slots):
    phase = fresnel_phase(N)
    kernel = lax.complex(phase[0], phase[1])
    total = GROUPS * TILES * P_CAP
    counter = jnp.arange(total, dtype=jnp.int32)
    group_index = counter // (TILES * P_CAP)
    slot_index = counter % P_CAP
    alive = (slot_index.reshape(GROUPS, TILES, P_CAP) < live_slots[:, :, None]).reshape(total)
    records = (
        group_index * TH + row_offsets.reshape(total),
        scan_tiles.reshape(total) * TW + column_offsets.reshape(total),
        measured.reshape(total, N, N),
        alive.astype(object_real.dtype),
    )
    transmission = lax.complex(object_real, object_imag)
    probe = lax.complex(probe_real, probe_imag)
    rate = PROBE_STEP / total
    for turn in range(ITERS):
        current_object = transmission
        current_probe = probe

        def visit(carry, record):
            grad_object, grad_probe = carry
            row_start, column_start, pattern, weight = record
            anchor = jnp.zeros((), jnp.int32)
            corner = (anchor, row_start.astype(jnp.int32), column_start.astype(jnp.int32))
            window = lax.dynamic_slice(current_object, corner, (SLICES, N, N))
            wave = current_probe
            entering = []
            far = wave
            for level in range(SLICES):
                entering.append(wave)
                leaving = wave * window[level]
                if level < SLICES - 1:
                    wave = jnp.fft.ifft2(kernel * jnp.fft.fft2(leaving, norm="ortho"), norm="ortho")
                else:
                    far = jnp.fft.fft2(leaving, norm="ortho")
            resid = (jnp.sum(far.real * far.real + far.imag * far.imag, axis=0) - pattern) * weight
            back = jnp.fft.ifft2(resid * far, norm="ortho")
            layer_grads = [None] * SLICES
            for level in reversed(range(SLICES)):
                layer_grads[level] = jnp.sum(jnp.conj(entering[level]) * back, axis=0)
                carried = jnp.conj(window[level]) * back
                if level > 0:
                    back = jnp.fft.ifft2(jnp.conj(kernel) * jnp.fft.fft2(carried, norm="ortho"), norm="ortho")
                else:
                    grad_probe = grad_probe + carried
            update = jnp.stack(layer_grads)
            present = lax.dynamic_slice(grad_object, corner, (SLICES, N, N))
            grad_object = lax.dynamic_update_slice(grad_object, present + update, corner)
            return (grad_object, grad_probe), weight

        scanned = lax.scan(visit, (jnp.zeros_like(current_object), jnp.zeros_like(current_probe)), records)
        grad_object, grad_probe = scanned[0]
        transmission = current_object - OBJECT_STEP * grad_object
        probe = current_probe - rate * grad_probe
    return transmission.real, transmission.imag, probe.real, probe.imag
```

```python
import math

import jax
import jax.numpy as jnp
import ml_dtypes
import numpy as np
from jax import lax
from jax.experimental import pallas as pl
from jax.experimental.pallas import tpu as pltpu
from jax.sharding import Mesh
from jax.sharding import PartitionSpec as P

ITERS = 2
FRESNEL = 20.0
OBJECT_STEP = 0.2
PROBE_STEP = 0.5
F32 = jnp.float32
BF16 = jnp.bfloat16
FIELDS = 4


def fourier_tables(width):
    index = np.arange(width)
    angle = 2.0 * math.pi / width * (index[:, None] * index[None, :] % width)
    cosine = np.cos(angle) / math.sqrt(width)
    sine = np.sin(angle) / math.sqrt(width)
    forward = np.block([[cosine, -sine], [sine, cosine]])

    def parts(table):
        table = table.astype(np.float32)
        high = table.astype(ml_dtypes.bfloat16)
        low = (table - high.astype(np.float32)).astype(ml_dtypes.bfloat16)
        return [high, high, low]

    return (
        np.concatenate(parts(forward), axis=0),
        np.concatenate(parts(forward.T), axis=1),
        np.concatenate(parts(forward.T), axis=0),
        np.concatenate(parts(forward), axis=1),
    )


def fresnel_phase(width):
    index = np.arange(width)
    signed = ((index + width // 2) % width - width // 2).astype(np.float64)
    phase = FRESNEL * (signed[:, None] ** 2 + signed[None, :] ** 2) / float(width * width)
    return np.stack([np.cos(phase), -np.sin(phase)]).astype(np.float32)


def product_of(first, second):
    return (first[0] * second[0] - first[1] * second[1], first[0] * second[1] + first[1] * second[0])


def conj_product(first, second):
    return (first[0] * second[0] + first[1] * second[1], first[0] * second[1] - first[1] * second[0])


def split(value):
    high = value.astype(BF16)
    return high, (value - high.astype(F32)).astype(BF16)


def interleaved(field, axis):
    real_high, real_low = split(field[0])
    imag_high, imag_low = split(field[1])
    return jnp.concatenate([real_high, imag_high, real_low, imag_low, real_high, imag_high], axis=axis)


def along_last(fields, table, width):
    rows = jnp.concatenate([interleaved(field, 1) for field in fields], axis=0)
    out = jnp.dot(rows, table, preferred_element_type=F32)
    return [
        (out[width * m : width * (m + 1), :width], out[width * m : width * (m + 1), width:])
        for m in range(len(fields))
    ]


def along_first(fields, table, width):
    columns = jnp.concatenate([interleaved(field, 0) for field in fields], axis=1)
    out = jnp.dot(table, columns, preferred_element_type=F32)
    return [
        (out[:width, width * m : width * (m + 1)], out[width:, width * m : width * (m + 1)])
        for m in range(len(fields))
    ]


def slots_kernel(
    info,
    forward_last,
    forward_first,
    inverse_last,
    inverse_first,
    phase,
    probe,
    tile_own,
    tile_peer,
    tile_next,
    *rest,
):
    patterns = rest[:6]
    grad_own, grad_peer, grad_next, grad_probe = rest[6:10]
    tiles, grads, entering, far, window, layer_grads, resid = rest[10:]
    modes, width = probe.shape[1], probe.shape[2]
    capacity = patterns[0].shape[0]
    core, first_tile = info[0], info[1]

    def forward(fields):
        return along_first(along_last(fields, forward_last[...], width), forward_first[...], width)

    def inverse(fields):
        return along_first(along_last(fields, inverse_last[...], width), inverse_first[...], width)

    tiles[core] = tile_own[...]
    tiles[1 - core] = tile_peer[...]
    tiles[2] = tile_next[...]
    grads[...] = jnp.zeros_like(grads)
    grad_probe[...] = jnp.zeros_like(grad_probe)
    lane = lax.broadcasted_iota(jnp.int32, (width, width), 1)

    def one_slot(place, source, slot):
        tile = info[place] - first_tile
        row = info[place + 1]
        column = info[place + 2]
        keep = lane >= column
        for k in range(4):
            left = tiles[tile, k, pl.ds(row, width), :]
            right = tiles[tile + 1, k, pl.ds(row, width), :]
            window[k] = pltpu.roll(jnp.where(keep, left, right), lax.rem(width - column, width), 1)
        for which in range(6):

            @pl.when(source == which)
            def _():
                resid[...] = -patterns[which][slot]

        first_layer = (window[0], window[2])
        second_layer = (window[1], window[3])
        propagator = (phase[0], phase[1])
        start = [(probe[0, m], probe[1, m]) for m in range(modes)]
        spectrum = forward([product_of(wave, first_layer) for wave in start])
        middle = inverse([product_of(propagator, wave) for wave in spectrum])
        for m in range(modes):
            entering[0, m] = middle[m][0]
            entering[1, m] = middle[m][1]
        spectrum = forward([product_of(wave, second_layer) for wave in middle])
        total = resid[...]
        for m in range(modes):
            far[0, m] = spectrum[m][0]
            far[1, m] = spectrum[m][1]
            total = total + (spectrum[m][0] * spectrum[m][0] + spectrum[m][1] * spectrum[m][1])
        resid[...] = total

        weight = resid[...]
        back = inverse([(far[0, m] * weight, far[1, m] * weight) for m in range(modes)])
        pieces = [conj_product((entering[0, m], entering[1, m]), back[m]) for m in range(modes)]
        layer_grads[1] = sum(piece[0] for piece in pieces)
        layer_grads[3] = sum(piece[1] for piece in pieces)
        spectrum = forward([conj_product(second_layer, wave) for wave in back])
        back = inverse([conj_product(propagator, wave) for wave in spectrum])
        pieces = [conj_product((probe[0, m], probe[1, m]), back[m]) for m in range(modes)]
        layer_grads[0] = sum(piece[0] for piece in pieces)
        layer_grads[2] = sum(piece[1] for piece in pieces)
        for m in range(modes):
            carried = conj_product(first_layer, back[m])
            grad_probe[0, m] = grad_probe[0, m] + carried[0]
            grad_probe[1, m] = grad_probe[1, m] + carried[1]
        for k in range(4):
            update = pltpu.roll(layer_grads[k], column, 1)
            left = grads[tile, k, pl.ds(row, width), :]
            grads[tile, k, pl.ds(row, width), :] = left + jnp.where(keep, update, 0.0)
            right = grads[tile + 1, k, pl.ds(row, width), :]
            grads[tile + 1, k, pl.ds(row, width), :] = right + jnp.where(keep, 0.0, update)

    def candidate(index, rank):
        device = lax.div(index, 2 * capacity)
        parity = lax.rem(lax.div(index, capacity), 2)
        slot = lax.rem(index, capacity)
        source = 3 * (parity ^ core) + device
        place = 2 + FIELDS * (capacity * source + slot)
        tile = info[place] - first_tile
        mine = (tile >= 0) & (tile < 2) & (slot < info[place + 3])

        @pl.when(mine & (lax.rem(rank, 2) == core))
        def _():
            one_slot(place, source, slot)

        return rank + mine.astype(jnp.int32)

    lax.fori_loop(0, 6 * capacity, candidate, jnp.zeros((), jnp.int32))
    grad_own[...] = grads[core]
    grad_peer[...] = grads[1 - core]
    grad_next[...] = grads[2]


def slot_gradients(info, tables, phase, probe, tiles, patterns):
    tile = jax.ShapeDtypeStruct(tiles[0].shape, F32)
    modes, width = probe.shape[1], probe.shape[2]
    scalars = pl.BlockSpec(memory_space=pltpu.SMEM)
    whole = pl.BlockSpec(memory_space=pltpu.VMEM)
    return pl.pallas_call(
        slots_kernel,
        out_shape=(tile, tile, tile, jax.ShapeDtypeStruct(probe.shape, F32)),
        in_specs=[scalars] + [whole] * (9 + len(patterns)),
        out_specs=(whole,) * 4,
        scratch_shapes=[
            pltpu.VMEM((3,) + tiles[0].shape, F32),
            pltpu.VMEM((3,) + tiles[0].shape, F32),
            pltpu.VMEM(probe.shape, F32),
            pltpu.VMEM(probe.shape, F32),
            pltpu.VMEM((4, width, width), F32),
            pltpu.VMEM((4, width, width), F32),
            pltpu.VMEM((width, width), F32),
        ],
        compiler_params=pltpu.CompilerParams(vmem_limit_bytes=56 << 20),
        cost_estimate=pl.CostEstimate(flops=20_000_000_000, bytes_accessed=10_000_000, transcendentals=0),
    )(info, *tables, phase, probe, *tiles, *patterns)


def swap(value):
    return lax.ppermute(value, "core", [(0, 1), (1, 0)])


def chip_shift(value, by):
    chips = lax.axis_size("chip")
    return lax.ppermute(value, "chip", [(i, i + by) for i in range(chips) if 0 <= i + by < chips])


def to_even_from(value, core):
    chips = lax.axis_size("chip")
    return lax.ppermute(value, ("chip", "core"), [(2 * i + core, 2 * i + 2) for i in range(chips - 1)])


def from_even_to(value, core):
    chips = lax.axis_size("chip")
    return lax.ppermute(value, ("chip", "core"), [(2 * i + 2, 2 * i + core) for i in range(chips - 1)])


def summed_over_devices(value):
    shape = value.shape
    width = shape[-1]
    core = lax.axis_index("core")
    chips = lax.axis_size("grp") * lax.axis_size("chip")
    halves = value.reshape(2, -1, width)
    half = lax.dynamic_index_in_dim(halves, core, 0, keepdims=False)
    half = half + swap(lax.dynamic_index_in_dim(halves, 1 - core, 0, keepdims=False))
    pieces = lax.all_to_all(half.reshape(chips, -1, width), ("grp", "chip"), 0, 0)
    piece = jnp.sum(pieces, axis=0)
    pieces = lax.all_to_all(jnp.broadcast_to(piece[None], (chips,) + piece.shape), ("grp", "chip"), 0, 0)
    half = pieces.reshape(-1, width)
    other = swap(half)
    low = jnp.where(core == 0, half, other)
    high = jnp.where(core == 0, other, half)
    return jnp.concatenate([low, high]).reshape(shape)


def local(
    object_real,
    object_imag,
    probe_real,
    probe_imag,
    measured,
    scan_tiles,
    row_offsets,
    column_offsets,
    live_slots,
):
    width = probe_real.shape[2]
    capacity = measured.shape[2]
    core = lax.axis_index("core")
    chip = lax.axis_index("chip")
    slots = lax.axis_size("grp") * lax.axis_size("chip") * lax.axis_size("core") * capacity
    probe_rate = PROBE_STEP / slots
    tables = [jnp.asarray(table) for table in fourier_tables(width)]
    phase = jnp.asarray(fresnel_phase(width))

    own = jnp.concatenate([object_real, object_imag])
    probe = jnp.stack([probe_real, probe_imag])
    live = jnp.broadcast_to(live_slots[0, 0], (capacity,))
    records = jnp.stack([scan_tiles[0, 0], row_offsets[0, 0], column_offsets[0, 0], live], axis=1)
    near_records = [chip_shift(records, 1), records, chip_shift(records, -1)]
    near_patterns = [chip_shift(measured[0, 0], 1), measured[0, 0], chip_shift(measured[0, 0], -1)]
    near_records = jnp.stack(near_records)
    place = jnp.stack([core, 2 * chip]).astype(jnp.int32)
    info = jnp.concatenate([place, near_records.reshape(-1), swap(near_records).reshape(-1)])
    patterns = near_patterns + [swap(pattern) for pattern in near_patterns]

    for turn in range(ITERS):
        following = from_even_to(own, 0) + from_even_to(own, 1)
        tiles = (own, swap(own), following)
        grad_own, grad_peer, grad_next, grad_probe = slot_gradients(info, tables, phase, probe, tiles, patterns)
        total = grad_own + swap(grad_peer) + to_even_from(grad_next, 0) + to_even_from(grad_next, 1)
        own = own - OBJECT_STEP * total
        probe = probe - probe_rate * summed_over_devices(grad_probe)
    slices = object_real.shape[0]
    return (own[:slices], own[slices:], probe[0], probe[1])


def solution(mesh):
    groups, tiles = mesh.devices.shape
    fine = Mesh(mesh.devices.reshape(groups, tiles // 2, 2), ("grp", "chip", "core"))
    tile = ("chip", "core")
    placed = (
        P(None, "grp", tile),
        P(None, "grp", tile),
        P(),
        P(),
        P("grp", tile, None, None, None),
        P("grp", tile, None),
        P("grp", tile, None),
        P("grp", tile, None),
        P("grp", tile),
    )
    return jax.shard_map(
        local,
        mesh=fine,
        in_specs=placed,
        out_specs=(P(None, "grp", tile), P(None, "grp", tile), P(), P()),
        check_vma=False,
    )
```

```python
import math

import jax
import jax.numpy as jnp
import ml_dtypes
import numpy as np
from jax import lax
from jax.experimental import pallas as pl
from jax.experimental.pallas import tpu as pltpu
from jax.sharding import Mesh
from jax.sharding import PartitionSpec as P

ITERS = 2
FRESNEL = 20.0
OBJECT_STEP = 0.2
PROBE_STEP = 0.5
F32 = jnp.float32
BF16 = jnp.bfloat16
FIELDS = 4


def transform_tables(width):
    index = np.arange(width)
    angle = 2.0 * math.pi / width * (index[:, None] * index[None, :] % width)
    dft = (np.cos(angle) - 1j * np.sin(angle)) / math.sqrt(width)
    signed = ((index + width // 2) % width - width // 2).astype(np.float64)
    phase = FRESNEL * signed**2 / float(width * width)
    spread = dft.conj() @ (np.exp(-1j * phase)[:, None] * dft)

    def parts(matrix):
        table = np.block([[matrix.real, matrix.imag], [-matrix.imag, matrix.real]]).astype(np.float32)
        high = table.astype(ml_dtypes.bfloat16)
        low = (table - high.astype(np.float32)).astype(ml_dtypes.bfloat16)
        return np.stack([high, low])

    return parts(dft), parts(dft.conj()), parts(spread), parts(spread.conj())


def product_of(first, second):
    return (first[0] * second[0] - first[1] * second[1], first[0] * second[1] + first[1] * second[0])


def conj_product(first, second):
    return (first[0] * second[0] + first[1] * second[1], first[0] * second[1] - first[1] * second[0])


def split(value):
    high = value.astype(BF16)
    return high, (value - high.astype(F32)).astype(BF16)


def joined(field, axis):
    real_high, real_low = split(field[0])
    imag_high, imag_low = split(field[1])
    return jnp.concatenate([real_high, imag_high], axis=axis), jnp.concatenate([real_low, imag_low], axis=axis)


def matmul(first, second):
    return jnp.dot(first, second, preferred_element_type=F32)


def along_last(fields, table, width):
    outs = []
    for field in fields:
        high, low = joined(field, 1)
        out = matmul(high, table[0]) + matmul(low, table[0]) + matmul(high, table[1])
        outs.append((out[:, :width], out[:, width:]))
    return outs


def along_first(fields, table, width):
    if len(fields) > 2:
        return along_first(fields[:2], table, width) + along_first(fields[2:], table, width)
    pairs = [joined(field, 0) for field in fields]
    high = jnp.concatenate([pair[0] for pair in pairs], axis=1)
    low = jnp.concatenate([pair[1] for pair in pairs], axis=1)
    out = matmul(table[0], high) + matmul(table[0], low) + matmul(table[1], high)
    return [
        (out[:width, width * m : width * (m + 1)], out[width:, width * m : width * (m + 1)])
        for m in range(len(fields))
    ]


def slots_kernel(
    info,
    forward_table,
    inverse_table,
    spread_table,
    adjoint_table,
    probe_real,
    probe_imag,
    *rest,
):
    own, peer, following = rest[0:2], rest[2:4], rest[4:6]
    patterns = rest[6:12]
    grad_own, grad_peer, grad_next, grad_mine, grad_theirs = rest[12:17]
    entering, far, window, layer_grads, resid, grad_probe = rest[17:]
    modes, width = probe_real.shape[0], probe_real.shape[1]
    capacity = patterns[0].shape[0] // width
    core, first_tile = info[0], info[1]

    def two_sided(fields, right, left):
        return along_first(along_last(fields, right, width), left, width)

    grad_own[...] = jnp.zeros_like(grad_own)
    grad_peer[...] = jnp.zeros_like(grad_peer)
    grad_next[...] = jnp.zeros_like(grad_next)
    grad_probe[...] = jnp.zeros_like(grad_probe)
    lane = lax.broadcasted_iota(jnp.int32, (width, width), 1)

    def for_tiles(tile, action):
        @pl.when((core == 0) & (tile == 0))
        def _():
            action((own, peer), (grad_own, grad_peer))

        @pl.when((core == 0) & (tile == 1))
        def _():
            action((peer, following), (grad_peer, grad_next))

        @pl.when((core == 1) & (tile == 0))
        def _():
            action((peer, own), (grad_peer, grad_own))

        @pl.when((core == 1) & (tile == 1))
        def _():
            action((own, following[::-1]), (grad_own, grad_next))

    def one_slot(place, source, slot):
        tile = info[place] - first_tile
        row = info[place + 1]
        column = info[place + 2]
        keep = lane >= column

        def read(tiles, grads):
            for k in range(4):
                left = tiles[0][k // 2][k % 2, pl.ds(row, width), :]
                right = tiles[1][k // 2][k % 2, pl.ds(row, width), :]
                window[k] = pltpu.roll(jnp.where(keep, left, right), lax.rem(width - column, width), 1)

        for_tiles(tile, read)
        for which in range(6):

            @pl.when(source == which)
            def _():
                resid[...] = -patterns[which][pl.ds(pl.multiple_of(slot * width, width), width), :]

        first_layer = (window[0], window[2])
        second_layer = (window[1], window[3])
        start = [(probe_real[m], probe_imag[m]) for m in range(modes)]
        middle = two_sided([product_of(wave, first_layer) for wave in start], spread_table, adjoint_table)
        for m in range(modes):
            entering[0, m] = middle[m][0]
            entering[1, m] = middle[m][1]
        spectrum = two_sided([product_of(wave, second_layer) for wave in middle], forward_table, inverse_table)
        total = resid[...]
        for m in range(modes):
            far[0, m] = spectrum[m][0]
            far[1, m] = spectrum[m][1]
            total = total + (spectrum[m][0] * spectrum[m][0] + spectrum[m][1] * spectrum[m][1])
        resid[...] = total

        weight = resid[...]
        weighted = [(far[0, m] * weight, far[1, m] * weight) for m in range(modes)]
        back = two_sided(weighted, inverse_table, forward_table)
        pieces = [conj_product((entering[0, m], entering[1, m]), back[m]) for m in range(modes)]
        layer_grads[1] = sum(piece[0] for piece in pieces)
        layer_grads[3] = sum(piece[1] for piece in pieces)
        back = two_sided([conj_product(second_layer, wave) for wave in back], adjoint_table, spread_table)
        pieces = [conj_product((probe_real[m], probe_imag[m]), back[m]) for m in range(modes)]
        layer_grads[0] = sum(piece[0] for piece in pieces)
        layer_grads[2] = sum(piece[1] for piece in pieces)
        for m in range(modes):
            carried = conj_product(first_layer, back[m])
            grad_probe[0, m] = grad_probe[0, m] + carried[0]
            grad_probe[1, m] = grad_probe[1, m] + carried[1]

        def add(tiles, grads):
            for k in range(4):
                update = pltpu.roll(layer_grads[k], column, 1)
                left = grads[0][k, pl.ds(row, width), :]
                grads[0][k, pl.ds(row, width), :] = left + jnp.where(keep, update, 0.0)
                right = grads[1][k, pl.ds(row, width), :]
                grads[1][k, pl.ds(row, width), :] = right + jnp.where(keep, 0.0, update)

        for_tiles(tile, add)

    def candidate(index, rank):
        device = lax.div(index, 2 * capacity)
        parity = lax.rem(lax.div(index, capacity), 2)
        slot = lax.rem(index, capacity)
        source = 3 * (parity ^ core) + device
        place = 2 + FIELDS * (capacity * source + slot)
        tile = info[place] - first_tile
        mine = (tile >= 0) & (tile < 2) & (slot < info[place + 3])

        @pl.when(mine & (lax.rem(rank, 2) == core))
        def _():
            one_slot(place, source, slot)

        return rank + mine.astype(jnp.int32)

    lax.fori_loop(0, 6 * capacity, candidate, jnp.zeros((), jnp.int32))
    grad_mine[...] = grad_probe[core].reshape(grad_mine.shape)
    grad_theirs[...] = grad_probe[1 - core].reshape(grad_theirs.shape)


def slot_gradients(info, tables, probe, tiles, patterns):
    slices, height, wide = tiles[0].shape
    modes, width = probe[0].shape[0], probe[0].shape[1]
    tile = jax.ShapeDtypeStruct((2 * slices, height, wide), F32)
    part = jax.ShapeDtypeStruct((modes * width, width), F32)
    scalars = pl.BlockSpec(memory_space=pltpu.SMEM)
    whole = pl.BlockSpec(memory_space=pltpu.VMEM)
    return pl.pallas_call(
        slots_kernel,
        out_shape=(tile, tile, tile, part, part),
        in_specs=[scalars] + [whole] * (6 + len(tiles) + len(patterns)),
        out_specs=(whole,) * 5,
        scratch_shapes=[
            pltpu.VMEM((2, modes, width, width), F32),
            pltpu.VMEM((2, modes, width, width), F32),
            pltpu.VMEM((4, width, width), F32),
            pltpu.VMEM((4, width, width), F32),
            pltpu.VMEM((width, width), F32),
            pltpu.VMEM((2, modes, width, width), F32),
        ],
        compiler_params=pltpu.CompilerParams(vmem_limit_bytes=56 << 20),
        cost_estimate=pl.CostEstimate(flops=20_000_000_000, bytes_accessed=10_000_000, transcendentals=0),
    )(info, *tables, *probe, *tiles, *patterns)


def swap(value):
    return lax.ppermute(value, "core", [(0, 1), (1, 0)])


def chip_shift(value, by):
    chips = lax.axis_size("chip")
    return lax.ppermute(value, "chip", [(i, i + by) for i in range(chips) if 0 <= i + by < chips])


def from_even_to(value, core):
    chips = lax.axis_size("chip")
    return lax.ppermute(value, ("chip", "core"), [(2 * i + 2, 2 * i + core) for i in range(chips - 1)])


def scattered_sum(mine, theirs):
    chips = lax.axis_size("grp") * lax.axis_size("chip")
    half = mine + swap(theirs)
    return lax.all_to_all(half.reshape(chips, -1, 4, half.shape[-1]), ("grp", "chip"), 0, 0)


def gathered_sum(pieces):
    piece = jnp.sum(pieces, axis=0)
    return lax.all_to_all(jnp.broadcast_to(piece[None], pieces.shape), ("grp", "chip"), 0, 0)


def local(
    object_real,
    object_imag,
    probe_real,
    probe_imag,
    measured,
    scan_tiles,
    row_offsets,
    column_offsets,
    live_slots,
):
    width = probe_real.shape[2]
    capacity = measured.shape[2]
    slices = object_real.shape[0]
    core = lax.axis_index("core")
    chip = lax.axis_index("chip")
    slots = lax.axis_size("grp") * lax.axis_size("chip") * lax.axis_size("core") * capacity
    probe_rate = PROBE_STEP / slots
    tables = [jnp.asarray(table) for table in transform_tables(width)]

    live = jnp.broadcast_to(live_slots[0, 0], (capacity,))
    records = jnp.stack([scan_tiles[0, 0], row_offsets[0, 0], column_offsets[0, 0], live], axis=1)
    records = records.reshape(1, -1).astype(F32)
    records = jnp.pad(records, ((0, 7), (0, width - records.shape[1])))
    sent = jnp.concatenate([measured[0, 0].reshape(capacity * width, width), records])
    own = (object_real, object_imag)
    next_part = from_even_to(object_real, 0) + from_even_to(object_imag, 1)
    near = [chip_shift(sent, 1), sent, chip_shift(sent, -1)]
    peer = [swap(part) for part in own]
    near = near + [swap(each) for each in near]
    following = (next_part, swap(next_part))
    records = [each[capacity * width, : FIELDS * capacity] for each in near]
    place = jnp.stack([core, 2 * chip]).astype(jnp.int32)
    info = jnp.concatenate([place] + [record.astype(jnp.int32) for record in records])

    probe = (probe_real, probe_imag)
    for turn in range(ITERS):
        tiles = (*own, *peer, *following)
        grads = slot_gradients(info, tables, probe, tiles, near)
        grad_own, grad_peer, grad_next, grad_mine, grad_theirs = grads
        pieces = scattered_sum(grad_mine, grad_theirs)
        sum_own = grad_own + swap(grad_peer)
        sum_next = grad_next + swap(grad_next)
        sum_peer = grad_peer + swap(grad_own)
        sum_even = jnp.where(core == 0, sum_own, sum_peer)
        from_before = chip_shift(sum_next, 1)
        from_after = chip_shift(sum_even, -1)
        sum_own = jnp.where(core == 0, sum_own + from_before, sum_own)
        sum_peer = jnp.where(core == 0, sum_peer, sum_peer + from_before)
        sum_next = sum_next + from_after

        def stepped(tile, grad):
            return (tile[0] - OBJECT_STEP * grad[:slices], tile[1] - OBJECT_STEP * grad[slices:])

        own = stepped(own, sum_own)
        if turn < ITERS - 1:
            peer = stepped(peer, sum_peer)
            low = jnp.where(core == 0, sum_next[:slices], sum_next[slices:])
            high = jnp.where(core == 0, sum_next[slices:], sum_next[:slices])
            following = stepped(following, jnp.concatenate([low, high]))
        half = gathered_sum(pieces).reshape(grad_mine.shape)
        half, own, peer, following = lax.optimization_barrier((half, own, peer, following))
        other = swap(half)
        sums = (jnp.where(core == 0, half, other), jnp.where(core == 0, other, half))
        probe = [part - probe_rate * total.reshape(part.shape) for part, total in zip(probe, sums)]
    return (*own, *probe)


def solution(mesh):
    groups, tiles = mesh.devices.shape
    fine = Mesh(mesh.devices.reshape(groups, tiles // 2, 2), ("grp", "chip", "core"))
    tile = ("chip", "core")
    placed = (
        P(None, "grp", tile),
        P(None, "grp", tile),
        P(),
        P(),
        P("grp", tile, None, None, None),
        P("grp", tile, None),
        P("grp", tile, None),
        P("grp", tile, None),
        P("grp", tile),
    )
    return jax.shard_map(
        local,
        mesh=fine,
        in_specs=placed,
        out_specs=(P(None, "grp", tile), P(None, "grp", tile), P(), P()),
        check_vma=False,
    )
```

```python
import functools
import math

import jax
import jax.numpy as jnp
import ml_dtypes
import numpy as np
from jax import lax
from jax.experimental import pallas as pl
from jax.experimental.pallas import tpu as pltpu
from jax.sharding import Mesh
from jax.sharding import PartitionSpec as P

ITERS = 2
FRESNEL = 20.0
OBJECT_STEP = 0.2
PROBE_STEP = 0.5
F32 = jnp.float32
BF16 = jnp.bfloat16
FIELDS = 4


def transform_tables(width):
    index = np.arange(width)
    angle = 2.0 * math.pi / width * (index[:, None] * index[None, :] % width)
    dft = (np.cos(angle) - 1j * np.sin(angle)) / math.sqrt(width)
    signed = ((index + width // 2) % width - width // 2).astype(np.float64)
    phase = FRESNEL * signed**2 / float(width * width)
    spread = dft.conj() @ (np.exp(-1j * phase)[:, None] * dft)

    def parts(matrix):
        table = np.block([[matrix.real, matrix.imag], [-matrix.imag, matrix.real]]).astype(np.float32)
        high = table.astype(ml_dtypes.bfloat16)
        low = (table - high.astype(np.float32)).astype(ml_dtypes.bfloat16)
        return np.stack([high, low])

    return parts(dft), parts(dft.conj()), parts(spread), parts(spread.conj())


def product_of(first, second):
    return (first[0] * second[0] - first[1] * second[1], first[0] * second[1] + first[1] * second[0])


def conj_product(first, second):
    return (first[0] * second[0] + first[1] * second[1], first[0] * second[1] - first[1] * second[0])


def split(value):
    high = value.astype(BF16)
    return high, (value - high.astype(F32)).astype(BF16)


def joined(field, axis):
    real_high, real_low = split(field[0])
    imag_high, imag_low = split(field[1])
    return jnp.concatenate([real_high, imag_high], axis=axis), jnp.concatenate([real_low, imag_low], axis=axis)


def matmul(first, second):
    return jnp.dot(first, second, preferred_element_type=F32)


def along_last(fields, table, width):
    outs = []
    for field in fields:
        high, low = joined(field, 1)
        out = matmul(high, table[0]) + matmul(low, table[0]) + matmul(high, table[1])
        outs.append((out[:, :width], out[:, width:]))
    return outs


def along_first(fields, table, width):
    pairs = [joined(field, 0) for field in fields]
    high = jnp.concatenate([pair[0] for pair in pairs], axis=1)
    low = jnp.concatenate([pair[1] for pair in pairs], axis=1)
    out = matmul(table[0], high) + matmul(table[0], low) + matmul(table[1], high)
    return [
        (out[:width, width * m : width * (m + 1)], out[width:, width * m : width * (m + 1)])
        for m in range(len(fields))
    ]


def slots_kernel(
    info,
    forward_table,
    inverse_table,
    spread_table,
    adjoint_table,
    probe_real,
    probe_imag,
    *rest,
    first,
    probe_rate,
    height,
):
    patterns, rest = rest[:6], rest[6:]
    inputs, rest = (rest[:6], rest[6:]) if first else (rest[:8], rest[8:])
    (grad_even, grad_odd, grad_next, grad_mine, grad_theirs), rest = rest[:5], rest[5:]
    entering, far, window, layer_grads, resid, grad_probe, pattern, arrived, *updated = rest
    modes, width = probe_real.shape[0], probe_real.shape[1]
    capacity = patterns[1].shape[0] // width
    core, first_tile = info[0], info[1]
    if first:
        own, peer, following = inputs[0:2], inputs[2:4], inputs[4:6]
    else:
        sum_mine, sum_other, *inputs = inputs
        even, odd, following = inputs[0:2], inputs[2:4], inputs[4:6]
        (extra,) = updated

        def update(sum_real, sum_imag):
            extra[0] = probe_real[...] - probe_rate * sum_real[...].reshape(probe_real.shape)
            extra[1] = probe_imag[...] - probe_rate * sum_imag[...].reshape(probe_imag.shape)

        @pl.when(core == 0)
        def _():
            update(sum_mine, sum_other)

        @pl.when(core == 1)
        def _():
            update(sum_other, sum_mine)

        probe_real, probe_imag = extra.at[0], extra.at[1]

    def two_sided(produce, right, left, consume):
        rows = [None] * modes

        def last(m):
            rows[m] = along_last([produce(m)], right, width)[0]

        def first(*group):
            for m, out in zip(group, along_first([rows[m] for m in group], left, width)):
                consume(m, out)

        for m in range(modes):
            last(m)
        for m in range(0, modes, 2):
            first(m, m + 1)

    grad_even[...] = jnp.zeros_like(grad_even)
    grad_odd[...] = jnp.zeros_like(grad_odd)
    grad_next[...] = jnp.zeros_like(grad_next)
    grad_probe[...] = jnp.zeros_like(grad_probe)
    lane = lax.broadcasted_iota(jnp.int32, (width, width), 1)

    def one_slot(place, source, slot):
        tile = info[place] - first_tile
        row = info[place + 1]
        column = info[place + 2]
        keep = lane >= column

        for which in range(6):

            @pl.when(source == which)
            def _():
                block = pl.ds(pl.multiple_of(slot * width, width), width)
                pltpu.make_async_copy(patterns[which].at[block], pattern, arrived).start()

        def read(left_tile, right_tile):
            for k in range(4):
                block = pl.ds((k % 2) * height + row, width)
                left = left_tile[k // 2][block, :]
                right = right_tile[k // 2][block, :]
                window[k] = pltpu.roll(jnp.where(keep, left, right), lax.rem(width - column, width), 1)

        if first:

            @pl.when((core == 0) & (tile == 0))
            def _():
                read(own, peer)

            @pl.when((core == 0) & (tile == 1))
            def _():
                read(peer, following)

            @pl.when((core == 1) & (tile == 0))
            def _():
                read(peer, own)

            @pl.when((core == 1) & (tile == 1))
            def _():
                read(own, following[::-1])

        else:

            @pl.when(tile == 0)
            def _():
                read(even, odd)

            @pl.when(tile == 1)
            def _():
                read(odd, following)

        resid[...] = jnp.zeros_like(resid)
        first_layer = (window[0], window[2])
        second_layer = (window[1], window[3])
        def illuminated(m):
            return product_of((probe_real[m], probe_imag[m]), first_layer)

        def keep_middle(m, wave):
            entering[0, m], entering[1, m] = wave

        two_sided(illuminated, spread_table, adjoint_table, keep_middle)

        def leaving(m):
            return product_of((entering[0, m], entering[1, m]), second_layer)

        def keep_far(m, wave):
            far[0, m], far[1, m] = wave
            resid[...] += wave[0] * wave[0] + wave[1] * wave[1]

        two_sided(leaving, forward_table, inverse_table, keep_far)

        pltpu.make_async_copy(patterns[0].at[pl.ds(0, width)], pattern, arrived).wait()
        resid[...] = resid[...] - pattern[...]

        def weighted(m):
            return far[0, m] * resid[...], far[1, m] * resid[...]

        def take_second(m, wave):
            piece = conj_product((entering[0, m], entering[1, m]), wave)
            layer_grads[1] = piece[0] if m == 0 else layer_grads[1] + piece[0]
            layer_grads[3] = piece[1] if m == 0 else layer_grads[3] + piece[1]
            far[0, m], far[1, m] = conj_product(second_layer, wave)

        two_sided(weighted, inverse_table, forward_table, take_second)

        def carried_back(m):
            return far[0, m], far[1, m]

        def take_first(m, wave):
            piece = conj_product((probe_real[m], probe_imag[m]), wave)
            layer_grads[0] = piece[0] if m == 0 else layer_grads[0] + piece[0]
            layer_grads[2] = piece[1] if m == 0 else layer_grads[2] + piece[1]
            carried = conj_product(first_layer, wave)
            grad_probe[0, m] += carried[0]
            grad_probe[1, m] += carried[1]

        two_sided(carried_back, adjoint_table, spread_table, take_first)

        def add(left_grad, right_grad):
            for k in range(4):
                shifted = pltpu.roll(layer_grads[k], column, 1)
                lower = k // 2 * 2 * height + (k % 2) * height + row
                left_grad[pl.ds(lower, width), :] += jnp.where(keep, shifted, 0.0)
                right_grad[pl.ds(lower, width), :] += jnp.where(keep, 0.0, shifted)

        @pl.when(tile == 0)
        def _():
            add(grad_even, grad_odd)

        @pl.when(tile == 1)
        def _():
            add(grad_odd, grad_next)

    def candidate(index, rank):
        device = lax.div(index, 2 * capacity)
        parity = lax.rem(lax.div(index, capacity), 2)
        slot = lax.rem(index, capacity)
        source = 3 * (parity ^ core) + device
        place = 2 + FIELDS * (capacity * source + slot)
        tile = info[place] - first_tile
        mine = (tile >= 0) & (tile < 2) & (slot < info[place + 3])

        @pl.when(mine & (lax.rem(rank, 2) == core))
        def _():
            one_slot(place, source, slot)

        return rank + mine.astype(jnp.int32)

    lax.fori_loop(0, 6 * capacity, candidate, jnp.zeros((), jnp.int32))
    grad_mine[...] = grad_probe[core].reshape(grad_mine.shape)
    grad_theirs[...] = grad_probe[1 - core].reshape(grad_theirs.shape)


def slot_gradients(info, tables, probe, patterns, tiles, sums=(), probe_rate=None):
    first = not sums
    rows, wide = tiles[0].shape
    modes, width = probe[0].shape[0], probe[0].shape[1]
    tile = pltpu.VMEM((2 * rows, wide), F32)
    part = pltpu.VMEM((modes * width, width), F32)
    scalars = pl.BlockSpec(memory_space=pltpu.SMEM)
    whole = pl.BlockSpec(memory_space=pltpu.VMEM)
    in_place = pl.BlockSpec(memory_space=pltpu.HBM)
    arguments, held = (tiles[:2], tiles[2:]) if first else ((), (*sums, *tiles))
    arguments = (*tables, *probe, *patterns, *arguments)
    operands = [pltpu.with_memory_space_constraint(each, pltpu.HBM) for each in arguments]
    operands += [pltpu.with_memory_space_constraint(each, pltpu.VMEM) for each in held]
    extra = [] if first else [pltpu.VMEM((2, modes, width, width), F32)]
    return pl.pallas_call(
        functools.partial(slots_kernel, first=first, probe_rate=probe_rate, height=rows // 2),
        out_shape=(tile, tile, tile, part, part),
        in_specs=[scalars] + [whole] * 6 + [in_place] * len(patterns) + [whole] * (len(operands) - 6 - len(patterns)),
        out_specs=(whole,) * 5,
        scratch_shapes=[
            pltpu.VMEM((2, modes, width, width), F32),
            pltpu.VMEM((2, modes, width, width), F32),
            pltpu.VMEM((4, width, width), F32),
            pltpu.VMEM((4, width, width), F32),
            pltpu.VMEM((width, width), F32),
            pltpu.VMEM((2, modes, width, width), F32),
            pltpu.VMEM((width, width), F32),
            pltpu.SemaphoreType.DMA,
            *extra,
        ],
        compiler_params=pltpu.CompilerParams(vmem_limit_bytes=48 << 20),
        cost_estimate=pl.CostEstimate(flops=20_000_000_000, bytes_accessed=10_000_000, transcendentals=0),
    )(info, *operands)


def swap(value):
    return lax.ppermute(value, "core", [(0, 1), (1, 0)])


def chip_shift(value, by):
    chips = lax.axis_size("chip")
    return lax.ppermute(value, "chip", [(i, i + by) for i in range(chips) if 0 <= i + by < chips])


def scattered_sum(half):
    chips = lax.axis_size("grp") * lax.axis_size("chip")
    return lax.all_to_all(half.reshape(chips, -1, 4, half.shape[-1]), ("grp", "chip"), 0, 0)


def gathered_sum(pieces):
    piece = jnp.sum(pieces, axis=0)
    return lax.all_to_all(jnp.broadcast_to(piece[None], pieces.shape), ("grp", "chip"), 0, 0)


def local(
    object_real,
    object_imag,
    probe_real,
    probe_imag,
    measured,
    scan_tiles,
    row_offsets,
    column_offsets,
    live_slots,
):
    width = probe_real.shape[2]
    capacity = measured.shape[2]
    core = lax.axis_index("core")
    chip = lax.axis_index("chip")
    slots = lax.axis_size("grp") * lax.axis_size("chip") * lax.axis_size("core") * capacity
    probe_rate = PROBE_STEP / slots
    tables = [jnp.asarray(table) for table in transform_tables(width)]

    own = tuple(part.reshape(-1, part.shape[-1]) for part in (object_real, object_imag))
    rows = own[0].shape[0]
    peer = tuple(swap(part) for part in own)
    live = jnp.broadcast_to(live_slots[0, 0], (capacity,))
    records = jnp.stack([scan_tiles[0, 0], row_offsets[0, 0], column_offsets[0, 0], live], axis=1)
    records = records.reshape(1, -1).astype(F32)
    records = jnp.pad(records, ((0, 7), (0, width - records.shape[1])))
    pattern = measured[0, 0].reshape(capacity * width, width)
    after = chip_shift(pattern, -1)
    sent = jnp.concatenate([pattern, records])
    before = chip_shift(sent, 1)
    part = chip_shift(jnp.concatenate([jnp.where(core == 0, own[0], peer[1]), records]), -1)
    near = [before, pattern, after, swap(before), swap(sent), swap(after)]
    following = (part, swap(part))
    records = [before[-8], records[0], part[-8], near[3][-8], near[4][-8], following[1][-8]]
    records = [record[: FIELDS * capacity].astype(jnp.int32) for record in records]
    place = jnp.stack([core, 2 * chip]).astype(jnp.int32)
    info = jnp.concatenate([place, *records])

    probe = (probe_real, probe_imag)
    sums = ()
    tiles = (*own, *peer, *following)
    for turn in range(ITERS):
        grads = slot_gradients(info, tables, probe, near, tiles, sums, probe_rate)
        grad_even, grad_odd, grad_next, grad_mine, grad_theirs = grads
        if sums:
            probe, sums, grad_mine = lax.optimization_barrier((probe, sums, grad_mine))
            probe = stepped_probe(probe, sums, core, probe_rate)
        else:
            following = [each[:rows] for each in following]
            tiles = (
                *(jnp.where(core == 0, mine, other) for mine, other in zip(own, peer)),
                *(jnp.where(core == 0, other, mine) for mine, other in zip(own, peer)),
                jnp.where(core == 0, following[0], following[1]),
                jnp.where(core == 0, following[1], following[0]),
            )
        half = grad_mine + swap(grad_theirs)
        pieces = scattered_sum(half)
        sum_even = grad_even + swap(grad_even)
        sum_odd = grad_odd + swap(grad_odd)
        sum_next = grad_next + swap(grad_next)
        total = (sum_even + chip_shift(sum_next, 1), sum_odd, sum_next + chip_shift(sum_even, -1))
        tiles = tuple(
            tiles[2 * k + part] - OBJECT_STEP * total[k][rows * part : rows * (part + 1)] for k in range(3) for part in range(2)
        )
        half = gathered_sum(pieces).reshape(half.shape)
        half, tiles = lax.optimization_barrier((half, tiles))
        sums = (half, swap(half))
    own = [jnp.where(core == 0, tiles[part], tiles[2 + part]).reshape(object_real.shape) for part in range(2)]
    return (*own, *stepped_probe(probe, sums, core, probe_rate))


def stepped_probe(probe, sums, core, probe_rate):
    mine, other = sums
    sums = (jnp.where(core == 0, mine, other), jnp.where(core == 0, other, mine))
    return tuple(part - probe_rate * total.reshape(part.shape) for part, total in zip(probe, sums))


def solution(mesh):
    groups, tiles = mesh.devices.shape
    fine = Mesh(mesh.devices.reshape(groups, tiles // 2, 2), ("grp", "chip", "core"))
    tile = ("chip", "core")
    placed = (
        P(None, "grp", tile),
        P(None, "grp", tile),
        P(),
        P(),
        P("grp", tile, None, None, None),
        P("grp", tile, None),
        P("grp", tile, None),
        P("grp", tile, None),
        P("grp", tile),
    )
    return jax.shard_map(
        local,
        mesh=fine,
        in_specs=placed,
        out_specs=(P(None, "grp", tile), P(None, "grp", tile), P(), P()),
        check_vma=False,
    )
```

```python
import functools
import math

import jax
import jax.numpy as jnp
import ml_dtypes
import numpy as np
from jax import lax
from jax.experimental import pallas as pl
from jax.experimental.pallas import tpu as pltpu
from jax.sharding import Mesh
from jax.sharding import PartitionSpec as P

ITERS = 2
FRESNEL = 20.0
OBJECT_STEP = 0.2
PROBE_STEP = 0.5
F32 = jnp.float32
BF16 = jnp.bfloat16
FIELDS = 4


def transform_tables(width):
    index = np.arange(width)
    angle = 2.0 * math.pi / width * (index[:, None] * index[None, :] % width)
    dft = (np.cos(angle) - 1j * np.sin(angle)) / math.sqrt(width)
    signed = ((index + width // 2) % width - width // 2).astype(np.float64)
    phase = FRESNEL * signed**2 / float(width * width)
    spread = dft.conj() @ (np.exp(-1j * phase)[:, None] * dft)

    def parts(matrix):
        table = np.block([[matrix.real, matrix.imag], [-matrix.imag, matrix.real]]).astype(np.float32)
        high = table.astype(ml_dtypes.bfloat16)
        low = (table - high.astype(np.float32)).astype(ml_dtypes.bfloat16)
        return np.stack([high, low])

    return parts(dft), parts(dft.conj()), parts(spread), parts(spread.conj())


def product_of(first, second):
    return (first[0] * second[0] - first[1] * second[1], first[0] * second[1] + first[1] * second[0])


def conj_product(first, second):
    return (first[0] * second[0] + first[1] * second[1], first[0] * second[1] - first[1] * second[0])


def split(value):
    high = value.astype(BF16)
    return high, (value - high.astype(F32)).astype(BF16)


def joined(field, axis):
    real_high, real_low = split(field[0])
    imag_high, imag_low = split(field[1])
    return jnp.concatenate([real_high, imag_high], axis=axis), jnp.concatenate([real_low, imag_low], axis=axis)


def matmul(first, second):
    return jnp.dot(first, second, preferred_element_type=F32)


def along_last(fields, table, width):
    outs = []
    for field in fields:
        high, low = joined(field, 1)
        out = matmul(high, table[0]) + matmul(low, table[0]) + matmul(high, table[1])
        outs.append((out[:, :width], out[:, width:]))
    return outs


def along_first(fields, table, width):
    pairs = [joined(field, 0) for field in fields]
    high = jnp.concatenate([pair[0] for pair in pairs], axis=1)
    low = jnp.concatenate([pair[1] for pair in pairs], axis=1)
    out = matmul(table[0], high) + matmul(table[0], low) + matmul(table[1], high)
    return [
        (out[:width, width * m : width * (m + 1)], out[width:, width * m : width * (m + 1)])
        for m in range(len(fields))
    ]


def slots_kernel(
    info,
    forward_table,
    inverse_table,
    spread_table,
    adjoint_table,
    probe_real,
    probe_imag,
    *rest,
    first,
    probe_rate,
    height,
):
    patterns, rest = rest[:6], rest[6:]
    inputs, rest = (rest[:6], rest[6:]) if first else (rest[:8], rest[8:])
    (grad_even, grad_odd, grad_next, grad_mine, grad_theirs), rest = rest[:5], rest[5:]
    entering, far, window, layer_grads, resid, grad_probe, pattern, arrived, mine, *updated = rest
    modes, width = probe_real.shape[0], probe_real.shape[1]
    capacity = patterns[1].shape[0] // width
    core, first_tile = info[0], info[1]
    if first:
        own, peer, following = inputs[0:2], inputs[2:4], inputs[4:6]
    else:
        sum_mine, sum_other, *inputs = inputs
        even, odd, following = inputs[0:2], inputs[2:4], inputs[4:6]
        (extra,) = updated

        def update(sum_real, sum_imag):
            extra[0] = probe_real[...] - probe_rate * sum_real[...].reshape(probe_real.shape)
            extra[1] = probe_imag[...] - probe_rate * sum_imag[...].reshape(probe_imag.shape)

        @pl.when(core == 0)
        def _():
            update(sum_mine, sum_other)

        @pl.when(core == 1)
        def _():
            update(sum_other, sum_mine)

        probe_real, probe_imag = extra.at[0], extra.at[1]

    def two_sided(items, produce, right, left, consume):
        rows = [along_last([produce(*item)], right, width)[0] for item in items]
        for k in range(0, len(items), 2):
            for item, out in zip(items[k : k + 2], along_first(rows[k : k + 2], left, width)):
                consume(*item, out)

    grad_even[...] = jnp.zeros_like(grad_even)
    grad_odd[...] = jnp.zeros_like(grad_odd)
    grad_next[...] = jnp.zeros_like(grad_next)
    grad_probe[...] = jnp.zeros_like(grad_probe)
    lane = lax.broadcasted_iota(jnp.int32, (width, width), 1)

    def read_window(tile, row, column, window):
        keep = lane >= column

        def read(left_tile, right_tile):
            for k in range(4):
                block = pl.ds((k % 2) * height + row, width)
                both = jnp.where(keep, left_tile[k // 2][block, :], right_tile[k // 2][block, :])
                window[k] = pltpu.roll(both, lax.rem(width - column, width), 1)

        if first:

            @pl.when((core == 0) & (tile == 0))
            def _():
                read(own, peer)

            @pl.when((core == 0) & (tile == 1))
            def _():
                read(peer, following)

            @pl.when((core == 1) & (tile == 0))
            def _():
                read(peer, own)

            @pl.when((core == 1) & (tile == 1))
            def _():
                read(own, following[::-1])

        else:

            @pl.when(tile == 0)
            def _():
                read(even, odd)

            @pl.when(tile == 1)
            def _():
                read(odd, following)

    def add_window(tile, row, column, layer_grad):
        keep = lane >= column

        def add(left_grad, right_grad):
            for k in range(4):
                shifted = pltpu.roll(layer_grad[k], column, 1)
                block = pl.ds(k * height + row, width)
                left_grad[block, :] += jnp.where(keep, shifted, 0.0)
                right_grad[block, :] += jnp.where(keep, 0.0, shifted)

        @pl.when(tile == 0)
        def _():
            add(grad_even, grad_odd)

        @pl.when(tile == 1)
        def _():
            add(grad_odd, grad_next)

    def some_slots(start, count):
        where = []
        for n in range(count):
            place, source, slot = (mine[field, start + n] for field in range(3))
            where.append((info[place] - first_tile, info[place + 1], info[place + 2]))
            for which in range(6):

                @pl.when(source == which)
                def _():
                    block = pl.ds(pl.multiple_of(slot * width, width), width)
                    pltpu.make_async_copy(patterns[which].at[block], pattern.at[n], arrived.at[n]).start()

        for n in range(count):
            read_window(*where[n], window.at[n])
        items = [(n, m) for m in range(modes) for n in range(count)]

        def illuminated(n, m):
            return product_of((probe_real[m], probe_imag[m]), (window[n, 0], window[n, 2]))

        def keep_middle(n, m, wave):
            entering[n, 0, m], entering[n, 1, m] = wave

        two_sided(items, illuminated, spread_table, adjoint_table, keep_middle)

        def leaving(n, m):
            return product_of((entering[n, 0, m], entering[n, 1, m]), (window[n, 1], window[n, 3]))

        def keep_far(n, m, wave):
            far[n, 0, m], far[n, 1, m] = wave
            power = wave[0] * wave[0] + wave[1] * wave[1]
            resid[n] = power if m == 0 else resid[n] + power

        two_sided(items, leaving, forward_table, inverse_table, keep_far)
        for n in range(count):
            pltpu.make_async_copy(patterns[0].at[pl.ds(0, width)], pattern.at[n], arrived.at[n]).wait()
            resid[n] = resid[n] - pattern[n]

        def weighted(n, m):
            return far[n, 0, m] * resid[n], far[n, 1, m] * resid[n]

        def accumulate(n, m, layer, piece):
            layer_grads[n, layer] = piece[0] if m == 0 else layer_grads[n, layer] + piece[0]
            layer_grads[n, 2 + layer] = piece[1] if m == 0 else layer_grads[n, 2 + layer] + piece[1]

        def take_second(n, m, wave):
            accumulate(n, m, 1, conj_product((entering[n, 0, m], entering[n, 1, m]), wave))
            far[n, 0, m], far[n, 1, m] = conj_product((window[n, 1], window[n, 3]), wave)

        two_sided(items, weighted, inverse_table, forward_table, take_second)

        def carried_back(n, m):
            return far[n, 0, m], far[n, 1, m]

        def take_first(n, m, wave):
            accumulate(n, m, 0, conj_product((probe_real[m], probe_imag[m]), wave))
            carried = conj_product((window[n, 0], window[n, 2]), wave)
            grad_probe[0, m] += carried[0]
            grad_probe[1, m] += carried[1]

        two_sided(items, carried_back, adjoint_table, spread_table, take_first)
        for n in range(count):
            add_window(*where[n], layer_grads.at[n])

    def candidate(index, rank):
        device = lax.div(index, 2 * capacity)
        parity = lax.rem(lax.div(index, capacity), 2)
        slot = lax.rem(index, capacity)
        source = 3 * (parity ^ core) + device
        place = 2 + FIELDS * (capacity * source + slot)
        tile = info[place] - first_tile
        taken = (tile >= 0) & (tile < 2) & (slot < info[place + 3])

        @pl.when(taken & (lax.rem(rank, 2) == core))
        def _():
            turn = lax.div(rank, 2)
            mine[0, turn] = place
            mine[1, turn] = source
            mine[2, turn] = slot

        return rank + taken.astype(jnp.int32)

    found = lax.fori_loop(0, 6 * capacity, candidate, jnp.zeros((), jnp.int32))
    number = lax.div(found + 1 - core, 2)

    def pair(index, _):
        some_slots(2 * index, 2)
        return 0

    lax.fori_loop(0, lax.div(number, 2), pair, 0)

    @pl.when(lax.rem(number, 2) == 1)
    def _():
        some_slots(number - 1, 1)

    grad_mine[...] = grad_probe[core].reshape(grad_mine.shape)
    grad_theirs[...] = grad_probe[1 - core].reshape(grad_theirs.shape)


def slot_gradients(info, tables, probe, patterns, tiles, sums=(), probe_rate=None):
    first = not sums
    rows, wide = tiles[0].shape
    modes, width = probe[0].shape[0], probe[0].shape[1]
    tile = pltpu.VMEM((2 * rows, wide), F32)
    part = pltpu.VMEM((modes * width, width), F32)
    scalars = pl.BlockSpec(memory_space=pltpu.SMEM)
    whole = pl.BlockSpec(memory_space=pltpu.VMEM)
    in_place = pl.BlockSpec(memory_space=pltpu.HBM)
    arguments, held = (tiles[:2], tiles[2:]) if first else ((), (*sums, *tiles))
    arguments = (*tables, *probe, *patterns, *arguments)
    operands = [pltpu.with_memory_space_constraint(each, pltpu.HBM) for each in arguments]
    operands += [pltpu.with_memory_space_constraint(each, pltpu.VMEM) for each in held]
    extra = [] if first else [pltpu.VMEM((2, modes, width, width), F32)]
    return pl.pallas_call(
        functools.partial(slots_kernel, first=first, probe_rate=probe_rate, height=rows // 2),
        out_shape=(tile, tile, tile, part, part),
        in_specs=[scalars] + [whole] * 6 + [in_place] * len(patterns) + [whole] * (len(operands) - 6 - len(patterns)),
        out_specs=(whole,) * 5,
        scratch_shapes=[
            pltpu.VMEM((2, 2, modes, width, width), F32),
            pltpu.VMEM((2, 2, modes, width, width), F32),
            pltpu.VMEM((2, 4, width, width), F32),
            pltpu.VMEM((2, 4, width, width), F32),
            pltpu.VMEM((2, width, width), F32),
            pltpu.VMEM((2, modes, width, width), F32),
            pltpu.VMEM((2, width, width), F32),
            pltpu.SemaphoreType.DMA((2,)),
            pltpu.SMEM((3, 3 * (patterns[1].shape[0] // width)), jnp.int32),
            *extra,
        ],
        compiler_params=pltpu.CompilerParams(vmem_limit_bytes=48 << 20),
        cost_estimate=pl.CostEstimate(flops=20_000_000_000, bytes_accessed=10_000_000, transcendentals=0),
    )(info, *operands)


def swap(value):
    return lax.ppermute(value, "core", [(0, 1), (1, 0)])


def chip_shift(value, by):
    chips = lax.axis_size("chip")
    return lax.ppermute(value, "chip", [(i, i + by) for i in range(chips) if 0 <= i + by < chips])


def scattered_sum(half):
    chips = lax.axis_size("grp") * lax.axis_size("chip")
    return lax.all_to_all(half.reshape(chips, -1, 4, half.shape[-1]), ("grp", "chip"), 0, 0)


def gathered_sum(pieces):
    piece = jnp.sum(pieces, axis=0)
    return lax.all_to_all(jnp.broadcast_to(piece[None], pieces.shape), ("grp", "chip"), 0, 0)


def local(
    object_real,
    object_imag,
    probe_real,
    probe_imag,
    measured,
    scan_tiles,
    row_offsets,
    column_offsets,
    live_slots,
):
    width = probe_real.shape[2]
    capacity = measured.shape[2]
    core = lax.axis_index("core")
    chip = lax.axis_index("chip")
    slots = lax.axis_size("grp") * lax.axis_size("chip") * lax.axis_size("core") * capacity
    probe_rate = PROBE_STEP / slots
    tables = [jnp.asarray(table) for table in transform_tables(width)]

    own = tuple(part.reshape(-1, part.shape[-1]) for part in (object_real, object_imag))
    rows = own[0].shape[0]
    peer = tuple(swap(part) for part in own)
    live = jnp.broadcast_to(live_slots[0, 0], (capacity,))
    records = jnp.stack([scan_tiles[0, 0], row_offsets[0, 0], column_offsets[0, 0], live], axis=1)
    records = records.reshape(1, -1).astype(F32)
    records = jnp.pad(records, ((0, 7), (0, width - records.shape[1])))
    pattern = measured[0, 0].reshape(capacity * width, width)
    after = chip_shift(pattern, -1)
    payload = jnp.concatenate([jnp.where(core == 0, own[0], peer[1]), records])
    sent = jnp.concatenate([pattern, records])
    payload, sent = lax.optimization_barrier((payload, sent))
    part = chip_shift(payload, -1)
    before = chip_shift(sent, 1)
    near = [before, pattern, after, swap(before), swap(sent), swap(after)]
    following = (part, swap(part))
    records = [before[-8], records[0], part[-8], near[3][-8], near[4][-8], following[1][-8]]
    records = [record[: FIELDS * capacity].astype(jnp.int32) for record in records]
    place = jnp.stack([core, 2 * chip]).astype(jnp.int32)
    info = jnp.concatenate([place, *records])

    probe = (probe_real, probe_imag)
    sums = ()
    tiles = (*own, *peer, *following)
    for turn in range(ITERS):
        grads = slot_gradients(info, tables, probe, near, tiles, sums, probe_rate)
        grad_even, grad_odd, grad_next, grad_mine, grad_theirs = grads
        if sums:
            probe, sums, grad_mine = lax.optimization_barrier((probe, sums, grad_mine))
            probe = stepped_probe(probe, sums, core, probe_rate)
        else:
            following = [each[:rows] for each in following]
            tiles = (
                *(jnp.where(core == 0, mine, other) for mine, other in zip(own, peer)),
                *(jnp.where(core == 0, other, mine) for mine, other in zip(own, peer)),
                jnp.where(core == 0, following[0], following[1]),
                jnp.where(core == 0, following[1], following[0]),
            )
        half = grad_mine + swap(grad_theirs)
        pieces = scattered_sum(half)
        sum_even = grad_even + swap(grad_even)
        sum_odd = grad_odd + swap(grad_odd)
        sum_next = grad_next + swap(grad_next)
        total = (sum_even + chip_shift(sum_next, 1), sum_odd, sum_next + chip_shift(sum_even, -1))
        tiles = tuple(
            tiles[2 * k + part] - OBJECT_STEP * total[k][rows * part : rows * (part + 1)] for k in range(3) for part in range(2)
        )
        half = gathered_sum(pieces).reshape(half.shape)
        if turn == ITERS - 1:
            tiles = tuple(jnp.where(core == 0, tiles[part], tiles[2 + part]) for part in range(2))
        half, tiles = lax.optimization_barrier((half, tiles))
        sums = (half, swap(half))
    own = [part.reshape(object_real.shape) for part in tiles]
    return (*own, *stepped_probe(probe, sums, core, probe_rate))


def stepped_probe(probe, sums, core, probe_rate):
    mine, other = sums
    sums = (jnp.where(core == 0, mine, other), jnp.where(core == 0, other, mine))
    return tuple(part - probe_rate * total.reshape(part.shape) for part, total in zip(probe, sums))


def solution(mesh):
    groups, tiles = mesh.devices.shape
    fine = Mesh(mesh.devices.reshape(groups, tiles // 2, 2), ("grp", "chip", "core"))
    tile = ("chip", "core")
    placed = (
        P(None, "grp", tile),
        P(None, "grp", tile),
        P(),
        P(),
        P("grp", tile, None, None, None),
        P("grp", tile, None),
        P("grp", tile, None),
        P("grp", tile, None),
        P("grp", tile),
    )
    return jax.shard_map(
        local,
        mesh=fine,
        in_specs=placed,
        out_specs=(P(None, "grp", tile), P(None, "grp", tile), P(), P()),
        check_vma=False,
    )
```

```python
import functools
import math

import jax
import jax.numpy as jnp
import ml_dtypes
import numpy as np
from jax import lax
from jax.experimental import pallas as pl
from jax.experimental.pallas import tpu as pltpu
from jax.sharding import Mesh
from jax.sharding import PartitionSpec as P

ITERS = 2
FRESNEL = 20.0
OBJECT_STEP = 0.2
PROBE_STEP = 0.5
F32 = jnp.float32
BF16 = jnp.bfloat16
FIELDS = 4


def transform_tables(width):
    index = np.arange(width)
    angle = 2.0 * math.pi / width * (index[:, None] * index[None, :] % width)
    dft = (np.cos(angle) - 1j * np.sin(angle)) / math.sqrt(width)
    signed = ((index + width // 2) % width - width // 2).astype(np.float64)
    phase = FRESNEL * signed**2 / float(width * width)
    spread = dft.conj() @ (np.exp(-1j * phase)[:, None] * dft)

    def parts(matrix):
        table = np.block([[matrix.real, matrix.imag], [-matrix.imag, matrix.real]]).astype(np.float32)
        high = table.astype(ml_dtypes.bfloat16)
        low = (table - high.astype(np.float32)).astype(ml_dtypes.bfloat16)
        return np.stack([high, low])

    return parts(dft), parts(dft.conj()), parts(spread), parts(spread.conj())


def product_of(first, second):
    return (first[0] * second[0] - first[1] * second[1], first[0] * second[1] + first[1] * second[0])


def conj_product(first, second):
    return (first[0] * second[0] + first[1] * second[1], first[0] * second[1] - first[1] * second[0])


def split(value):
    high = value.astype(BF16)
    return high, (value - high.astype(F32)).astype(BF16)


def joined(field, axis):
    real_high, real_low = split(field[0])
    imag_high, imag_low = split(field[1])
    return jnp.concatenate([real_high, imag_high], axis=axis), jnp.concatenate([real_low, imag_low], axis=axis)


def matmul(first, second):
    return jnp.dot(first, second, preferred_element_type=F32)


def along_last(fields, table, width):
    outs = []
    for field in fields:
        high, low = joined(field, 1)
        out = matmul(high, table[0]) + matmul(low, table[0]) + matmul(high, table[1])
        outs.append((out[:, :width], out[:, width:]))
    return outs


def along_first(fields, table, width):
    pairs = [joined(field, 0) for field in fields]
    high = jnp.concatenate([pair[0] for pair in pairs], axis=1)
    low = jnp.concatenate([pair[1] for pair in pairs], axis=1)
    out = matmul(table[0], high) + matmul(table[0], low) + matmul(table[1], high)
    return [
        (out[:width, width * m : width * (m + 1)], out[width:, width * m : width * (m + 1)])
        for m in range(len(fields))
    ]


def slots_kernel(
    info,
    forward_table,
    inverse_table,
    spread_table,
    adjoint_table,
    probe_real,
    probe_imag,
    *rest,
    first,
    probe_rate,
    height,
):
    patterns, rest = rest[:6], rest[6:]
    inputs, rest = (rest[:6], rest[6:]) if first else (rest[:8], rest[8:])
    (grad_even, grad_odd, grad_next, grad_mine, grad_theirs), rest = rest[:5], rest[5:]
    entering, far, window, layer_grads, resid, grad_probe, pattern, arrived, mine, *updated = rest
    modes, width = probe_real.shape[0], probe_real.shape[1]
    capacity = patterns[1].shape[0] // width
    core, first_tile = info[0], info[1]
    if first:
        own, peer, following = inputs[0:2], inputs[2:4], inputs[4:6]
    else:
        sum_mine, sum_other, *inputs = inputs
        even, odd, following = inputs[0:2], inputs[2:4], inputs[4:6]
        (extra,) = updated

        def update(sum_real, sum_imag):
            extra[0] = probe_real[...] - probe_rate * sum_real[...].reshape(probe_real.shape)
            extra[1] = probe_imag[...] - probe_rate * sum_imag[...].reshape(probe_imag.shape)

        @pl.when(core == 0)
        def _():
            update(sum_mine, sum_other)

        @pl.when(core == 1)
        def _():
            update(sum_other, sum_mine)

        probe_real, probe_imag = extra.at[0], extra.at[1]

    def two_sided(items, produce, right, left, consume):
        rows = [along_last([produce(*item)], right, width)[0] for item in items]
        for k in range(0, len(items), 2):
            for item, out in zip(items[k : k + 2], along_first(rows[k : k + 2], left, width)):
                consume(*item, out)

    grad_even[...] = jnp.zeros_like(grad_even)
    grad_odd[...] = jnp.zeros_like(grad_odd)
    grad_next[...] = jnp.zeros_like(grad_next)
    grad_probe[...] = jnp.zeros_like(grad_probe)
    lane = lax.broadcasted_iota(jnp.int32, (width, width), 1)

    def read_window(tile, row, column, window):
        keep = lane >= column

        def read(left_tile, right_tile):
            for k in range(4):
                block = pl.ds((k % 2) * height + row, width)
                both = jnp.where(keep, left_tile[k // 2][block, :], right_tile[k // 2][block, :])
                window[k] = pltpu.roll(both, lax.rem(width - column, width), 1)

        if first:

            @pl.when((core == 0) & (tile == 0))
            def _():
                read(own, peer)

            @pl.when((core == 0) & (tile == 1))
            def _():
                read(peer, following)

            @pl.when((core == 1) & (tile == 0))
            def _():
                read(peer, own)

            @pl.when((core == 1) & (tile == 1))
            def _():
                read(own, following[::-1])

        else:

            @pl.when(tile == 0)
            def _():
                read(even, odd)

            @pl.when(tile == 1)
            def _():
                read(odd, following)

    def add_window(tile, row, column, layer_grad):
        keep = lane >= column

        def add(left_grad, right_grad):
            for k in range(4):
                shifted = pltpu.roll(layer_grad[k], column, 1)
                block = pl.ds(k * height + row, width)
                left_grad[block, :] += jnp.where(keep, shifted, 0.0)
                right_grad[block, :] += jnp.where(keep, 0.0, shifted)

        @pl.when(tile == 0)
        def _():
            add(grad_even, grad_odd)

        @pl.when(tile == 1)
        def _():
            add(grad_odd, grad_next)

    def some_slots(start, count):
        where = []
        for n in range(count):
            place, source, slot = (mine[field, start + n] for field in range(3))
            where.append((info[place] - first_tile, info[place + 1], info[place + 2]))
            for which in range(6):

                @pl.when(source == which)
                def _():
                    block = pl.ds(pl.multiple_of(slot * width, width), width)
                    pltpu.make_async_copy(patterns[which].at[block], pattern.at[n], arrived.at[n]).start()

        for n in range(count):
            read_window(*where[n], window.at[n])
        items = [(n, m) for m in range(modes) for n in range(count)]

        def illuminated(n, m):
            return product_of((probe_real[m], probe_imag[m]), (window[n, 0], window[n, 2]))

        def keep_middle(n, m, wave):
            entering[n, 0, m], entering[n, 1, m] = wave

        two_sided(items, illuminated, spread_table, adjoint_table, keep_middle)

        def leaving(n, m):
            return product_of((entering[n, 0, m], entering[n, 1, m]), (window[n, 1], window[n, 3]))

        def keep_far(n, m, wave):
            far[n, 0, m], far[n, 1, m] = wave
            power = wave[0] * wave[0] + wave[1] * wave[1]
            resid[n] = power if m == 0 else resid[n] + power

        two_sided(items, leaving, forward_table, inverse_table, keep_far)
        for n in range(count):
            pltpu.make_async_copy(patterns[0].at[pl.ds(0, width)], pattern.at[n], arrived.at[n]).wait()
            resid[n] = resid[n] - pattern[n]

        def weighted(n, m):
            return far[n, 0, m] * resid[n], far[n, 1, m] * resid[n]

        def accumulate(n, m, layer, piece):
            layer_grads[n, layer] = piece[0] if m == 0 else layer_grads[n, layer] + piece[0]
            layer_grads[n, 2 + layer] = piece[1] if m == 0 else layer_grads[n, 2 + layer] + piece[1]

        def take_second(n, m, wave):
            accumulate(n, m, 1, conj_product((entering[n, 0, m], entering[n, 1, m]), wave))
            far[n, 0, m], far[n, 1, m] = conj_product((window[n, 1], window[n, 3]), wave)

        two_sided(items, weighted, inverse_table, forward_table, take_second)

        def carried_back(n, m):
            return far[n, 0, m], far[n, 1, m]

        def take_first(n, m, wave):
            accumulate(n, m, 0, conj_product((probe_real[m], probe_imag[m]), wave))
            carried = conj_product((window[n, 0], window[n, 2]), wave)
            grad_probe[0, m] += carried[0]
            grad_probe[1, m] += carried[1]

        two_sided(items, carried_back, adjoint_table, spread_table, take_first)
        for n in range(count):
            add_window(*where[n], layer_grads.at[n])

    def candidate(index, rank):
        device = lax.div(index, 2 * capacity)
        parity = lax.rem(lax.div(index, capacity), 2)
        slot = lax.rem(index, capacity)
        source = 3 * (parity ^ core) + device
        place = 2 + FIELDS * (capacity * source + slot)
        tile = info[place] - first_tile
        taken = (tile >= 0) & (tile < 2) & (slot < info[place + 3])

        @pl.when(taken & (lax.rem(rank, 2) == core))
        def _():
            turn = lax.div(rank, 2)
            mine[0, turn] = place
            mine[1, turn] = source
            mine[2, turn] = slot

        return rank + taken.astype(jnp.int32)

    found = lax.fori_loop(0, 6 * capacity, candidate, jnp.zeros((), jnp.int32), unroll=True)
    number = lax.div(found + 1 - core, 2)

    def pair(index, _):
        some_slots(2 * index, 2)
        return 0

    lax.fori_loop(0, lax.div(number, 2), pair, 0)

    @pl.when(lax.rem(number, 2) == 1)
    def _():
        some_slots(number - 1, 1)

    grad_mine[...] = grad_probe[core].reshape(grad_mine.shape)
    grad_theirs[...] = grad_probe[1 - core].reshape(grad_theirs.shape)


def slot_gradients(info, tables, probe, patterns, tiles, sums=(), probe_rate=None):
    first = not sums
    rows, wide = tiles[0].shape
    modes, width = probe[0].shape[0], probe[0].shape[1]
    tile = pltpu.VMEM((2 * rows, wide), F32)
    part = pltpu.VMEM((modes * width, width), F32)
    scalars = pl.BlockSpec(memory_space=pltpu.SMEM)
    whole = pl.BlockSpec(memory_space=pltpu.VMEM)
    in_place = pl.BlockSpec(memory_space=pltpu.HBM)
    in_vmem = [first and k != 1 for k in range(len(patterns))]
    placed = [(each, pltpu.HBM) for each in (*tables, *probe)]
    placed += [(each, pltpu.VMEM if here else pltpu.HBM) for each, here in zip(patterns, in_vmem)]
    placed += [(each, pltpu.HBM if first and k < 2 else pltpu.VMEM) for k, each in enumerate((*sums, *tiles))]
    operands = [pltpu.with_memory_space_constraint(*each) for each in placed]
    extra = [] if first else [pltpu.VMEM((2, modes, width, width), F32)]
    return pl.pallas_call(
        functools.partial(slots_kernel, first=first, probe_rate=probe_rate, height=rows // 2),
        out_shape=(tile, tile, tile, part, part),
        in_specs=[scalars] + [whole] * 6 + [whole if here else in_place for here in in_vmem] + [whole] * (len(operands) - 6 - len(patterns)),
        out_specs=(whole,) * 5,
        scratch_shapes=[
            pltpu.VMEM((2, 2, modes, width, width), F32),
            pltpu.VMEM((2, 2, modes, width, width), F32),
            pltpu.VMEM((2, 4, width, width), F32),
            pltpu.VMEM((2, 4, width, width), F32),
            pltpu.VMEM((2, width, width), F32),
            pltpu.VMEM((2, modes, width, width), F32),
            pltpu.VMEM((2, width, width), F32),
            pltpu.SemaphoreType.DMA((2,)),
            pltpu.SMEM((3, 3 * (patterns[1].shape[0] // width)), jnp.int32),
            *extra,
        ],
        compiler_params=pltpu.CompilerParams(vmem_limit_bytes=48 << 20),
        cost_estimate=pl.CostEstimate(flops=20_000_000_000, bytes_accessed=10_000_000, transcendentals=0),
    )(info, *operands)


def swap(value):
    return lax.ppermute(value, "core", [(0, 1), (1, 0)])


def chip_shift(value, by):
    chips = lax.axis_size("chip")
    return lax.ppermute(value, "chip", [(i, i + by) for i in range(chips) if 0 <= i + by < chips])


def scattered_sum(half):
    chips = lax.axis_size("grp") * lax.axis_size("chip")
    return lax.all_to_all(half.reshape(chips, -1, 4, half.shape[-1]), ("grp", "chip"), 0, 0)


def gathered_sum(pieces):
    piece = jnp.sum(pieces, axis=0)
    return lax.all_to_all(jnp.broadcast_to(piece[None], pieces.shape), ("grp", "chip"), 0, 0)


def local(
    object_real,
    object_imag,
    probe_real,
    probe_imag,
    measured,
    scan_tiles,
    row_offsets,
    column_offsets,
    live_slots,
):
    width = probe_real.shape[2]
    capacity = measured.shape[2]
    core = lax.axis_index("core")
    chip = lax.axis_index("chip")
    slots = lax.axis_size("grp") * lax.axis_size("chip") * lax.axis_size("core") * capacity
    probe_rate = PROBE_STEP / slots
    tables = [jnp.asarray(table) for table in transform_tables(width)]

    own = tuple(part.reshape(-1, part.shape[-1]) for part in (object_real, object_imag))
    rows = own[0].shape[0]
    peer = tuple(swap(part) for part in own)
    live = jnp.broadcast_to(live_slots[0, 0], (capacity,))
    records = jnp.stack([scan_tiles[0, 0], row_offsets[0, 0], column_offsets[0, 0], live], axis=1)
    records = records.reshape(1, -1).astype(F32)
    records = jnp.pad(records, ((0, 7), (0, width - records.shape[1])))
    pattern = measured[0, 0].reshape(capacity * width, width)
    after = chip_shift(pattern, -1)
    payload = jnp.concatenate([jnp.where(core == 0, own[0], peer[1]), records])
    sent = jnp.concatenate([pattern, records])
    payload, sent = lax.optimization_barrier((payload, sent))
    part = chip_shift(payload, -1)
    before = chip_shift(sent, 1)
    near = [before, pattern, after, swap(before), swap(sent), swap(after)]
    following = (part, swap(part))
    records = [before[-8], records[0], part[-8], near[3][-8], near[4][-8], following[1][-8]]
    records = [record[: FIELDS * capacity].astype(jnp.int32) for record in records]
    place = jnp.stack([core, 2 * chip]).astype(jnp.int32)
    info = jnp.concatenate([place, *records])

    probe = (probe_real, probe_imag)
    sums = ()
    tiles = (*own, *peer, *following)
    for turn in range(ITERS):
        grads = slot_gradients(info, tables, probe, near, tiles, sums, probe_rate)
        grad_even, grad_odd, grad_next, grad_mine, grad_theirs = grads
        if sums:
            probe, sums, grad_mine = lax.optimization_barrier((probe, sums, grad_mine))
            probe = stepped_probe(probe, sums, core, probe_rate)
        else:
            following = [each[:rows] for each in following]
            tiles = (
                *(jnp.where(core == 0, mine, other) for mine, other in zip(own, peer)),
                *(jnp.where(core == 0, other, mine) for mine, other in zip(own, peer)),
                jnp.where(core == 0, following[0], following[1]),
                jnp.where(core == 0, following[1], following[0]),
            )
        half = grad_mine + swap(grad_theirs)
        pieces = scattered_sum(half)
        sum_even = grad_even + swap(grad_even)
        sum_odd = grad_odd + swap(grad_odd)
        sum_next = grad_next + swap(grad_next)
        total = (sum_even + chip_shift(sum_next, 1), sum_odd, sum_next + chip_shift(sum_even, -1))
        tiles = tuple(
            tiles[2 * k + part] - OBJECT_STEP * total[k][rows * part : rows * (part + 1)] for k in range(3) for part in range(2)
        )
        half = gathered_sum(pieces).reshape(half.shape)
        if turn == ITERS - 1:
            tiles = tuple(jnp.where(core == 0, tiles[part], tiles[2 + part]) for part in range(2))
        half, tiles = lax.optimization_barrier((half, tiles))
        sums = (half, swap(half))
    own = [part.reshape(object_real.shape) for part in tiles]
    return (*own, *stepped_probe(probe, sums, core, probe_rate))


def stepped_probe(probe, sums, core, probe_rate):
    mine, other = sums
    sums = (jnp.where(core == 0, mine, other), jnp.where(core == 0, other, mine))
    return tuple(part - probe_rate * total.reshape(part.shape) for part, total in zip(probe, sums))


def solution(mesh):
    groups, tiles = mesh.devices.shape
    fine = Mesh(mesh.devices.reshape(groups, tiles // 2, 2), ("grp", "chip", "core"))
    tile = ("chip", "core")
    placed = (
        P(None, "grp", tile),
        P(None, "grp", tile),
        P(),
        P(),
        P("grp", tile, None, None, None),
        P("grp", tile, None),
        P("grp", tile, None),
        P("grp", tile, None),
        P("grp", tile),
    )
    return jax.shard_map(
        local,
        mesh=fine,
        in_specs=placed,
        out_specs=(P(None, "grp", tile), P(None, "grp", tile), P(), P()),
        check_vma=False,
    )
```
